128 devices in a mesh: dp: 8 (over y, x_hi), ctx: 16 (over x_lo, z, core).
Axes of the slice: x: 4 (x_hi: 2, x_lo: 2; x = x_hi * 2 + x_lo), y: 4, z: 4, core: 2. Of those that a mesh axis runs over, the one named last changes fastest.
Arguments:
- signal: bfloat16 [8, 2048, 4096], P('dp', 'ctx'), may hold values from -6 to 6
- gate: bfloat16 [8, 2048, 4096], P('dp', 'ctx'), may hold values from -6 to 6
- cotangent: bfloat16 [8, 2048, 4096], P('dp', 'ctx'), may hold values from -6 to 6
- filter_taps: float32 [2048, 4096], P(None, 'ctx'), may hold values from -4 to 4
Outputs:
- signal_grad: bfloat16 [8, 2048, 4096], P('dp', 'ctx')
- gate_grad: bfloat16 [8, 2048, 4096], P('dp', 'ctx')
- taps_grad: float32 [2048, 4096], P('dp', 'ctx')
The draws below stay inside these ranges and needn't reach their ends.
All inputs are finite; a program needn't handle non-finite values.
Results may differ from the reference program's by a relative error of at most 0.019.
Values may be sent and summed in bfloat16 or wider, within the bound.
No kernel may reach another device: no remote copies, remote signals or barrier semaphores. Data moves between devices by JAX's collectives and lax.ppermute only.
A program may use at most 128 MiB of HBM per device.

```python
import math
import jax
import jax.numpy as jnp
from jax import lax

C = 4096
LENGTH = 2048
SEQS = 8


def draw_filter_taps(key, part):
    key = jax.random.fold_in(key, 7)
    key_values, key_rates = jax.random.split(key)
    position = jnp.arange(LENGTH, dtype=jnp.float32)[:, None]
    values = jnp.clip(jax.random.normal(key_values, (LENGTH, C), jnp.float32), -4.0, 4.0)
    log_rate = jax.random.uniform(key_rates, (1, C), jnp.float32, math.log(0.3 / LENGTH), math.log(1.0 / 30.0))
    envelope = jnp.exp(-jnp.exp(log_rate) * position)
    return values * envelope


def steps_of(key, extent, cuts, least, high):
    gain, own = 1.0, jax.random.fold_in(key, 6)
    for dim, parts in cuts:
        draws = jnp.exp(jax.random.uniform(jax.random.fold_in(own, dim), (parts,), jnp.float32, least / len(cuts), high / len(cuts)))
        gain = gain * jnp.repeat(draws, extent[dim] // parts).reshape([-1 if axis == dim else 1 for axis in range(len(extent))])
    return gain


def noise(stream_key, shape, scale, most, shards=(), held_as=jnp.bfloat16):
    array = jax.random.normal(stream_key, shape, jnp.float32) * scale
    if len(shards) > 0:
        array = steps_of(stream_key, shape, shards, -0.22, 0.18) * array
    return jnp.clip(array, min=-most, max=most).astype(held_as)


def setup_inputs(seed: int = 0) -> dict:
    splits = jax.random.split(jax.random.key(seed), 5)
    return {
        "signal": noise(splits[0], (SEQS, LENGTH, C), 1.0, 6.0, ((0, 8), (1, 16))),
        "gate": noise(splits[1], (SEQS, LENGTH, C), 1.0, 6.0, ((0, 8), (1, 16))),
        "cotangent": noise(splits[2], (SEQS, LENGTH, C), 1.0, 6.0, ((0, 8), (1, 16))),
        "filter_taps": draw_filter_taps(jax.random.fold_in(splits[4], 71), 0),
    }


def reference(signal, gate, cotangent, filter_taps):
    total = 2 * LENGTH
    scale = 1.0 / math.sqrt(LENGTH)
    taps = filter_taps * scale
    taps_spec = jnp.fft.rfft(taps, n=total, axis=0)

    def one_sequence(carry, fields):
        seq_signal, seq_gate, seq_cotangent = fields
        signal_spec = jnp.fft.rfft(seq_signal.astype(jnp.float32), n=total, axis=0)
        conv = jnp.fft.irfft(taps_spec * signal_spec, n=total, axis=0)[:LENGTH].astype(jnp.bfloat16)
        gate_grad = (seq_cotangent.astype(jnp.float32) * conv.astype(jnp.float32)).astype(jnp.bfloat16)
        product = (seq_cotangent.astype(jnp.float32) * seq_gate.astype(jnp.float32)).astype(jnp.bfloat16)
        product_spec = jnp.fft.rfft(product.astype(jnp.float32), n=total, axis=0)
        signal_grad = jnp.fft.irfft(jnp.conj(taps_spec) * product_spec, n=total, axis=0)[:LENGTH].astype(jnp.bfloat16)
        taps_term = jnp.fft.irfft(jnp.conj(signal_spec) * product_spec, n=total, axis=0)[:LENGTH] * scale
        return (carry + taps_term, (signal_grad, gate_grad))
    start = jnp.zeros((LENGTH, C), jnp.float32)
    taps_total, outputs = lax.scan(one_sequence, start, (signal, gate, cotangent))
    return (outputs[0], outputs[1], taps_total)
```

```python
import functools
import math

import jax
import jax.numpy as jnp
import ml_dtypes
import numpy as np
from jax import lax
from jax.experimental import pallas as pl
from jax.experimental.pallas import tpu as pltpu
from jax.sharding import PartitionSpec as P

F32 = jnp.float32
BF16 = jnp.bfloat16
RADIX = 16
INNER = 256
TOTAL = RADIX * INNER
BLOCKS = RADIX // 2
ROOT_HALF = math.sqrt(0.5)
COS_EIGHTH = math.cos(math.pi / 8)
SIN_EIGHTH = math.sin(math.pi / 8)
ROWS = 16
LANES = 128


def section_tables():
    column = np.arange(INNER)[None, :]
    forward = np.zeros((BLOCKS, 2 * INNER, 2 * INNER))
    half = INNER // 2
    row = np.arange(half)[:, None]
    for section in range(2):
        angle = 2 * np.pi * ((column * (RADIX * row + BLOCKS * section)) % TOTAL) / TOTAL
        place = slice(section * INNER, (section + 1) * INNER)
        forward[0, section * half : (section + 1) * half, place] = np.cos(angle)
        forward[0, INNER + section * half : INNER + (section + 1) * half, place] = -np.sin(angle)
    forward[0, INNER, :INNER] = np.cos(np.pi * column[0])
    row = np.arange(INNER)[:, None]
    for j in range(1, BLOCKS):
        angle = 2 * np.pi * ((column * (RADIX * row + j)) % TOTAL) / TOTAL
        forward[j] = np.block([[np.cos(angle), np.sin(angle)], [-np.sin(angle), np.cos(angle)]])
    weight = np.full((BLOCKS, 2 * INNER, 1), 2.0 / TOTAL)
    weight[0, 0] = weight[0, INNER] = 1.0 / TOTAL
    inverse = np.swapaxes(forward * weight, 1, 2)
    return (forward.astype(ml_dtypes.bfloat16), inverse.astype(ml_dtypes.bfloat16))


def half_sections(y0, y2, y4, y6):
    t, q = ROOT_HALF * (y2 - y6), ROOT_HALF * (y2 + y6)
    return (y0 + t, -(y4 + q)), (y0 - t, y4 - q)


def sections(x):
    x0, x1, x2, x3, x4, x5, x6, x7 = x
    a0, b0, a1, b1 = x0 + x4, x0 - x4, x1 + x5, x1 - x5
    a2, b2, a3, b3 = x2 + x6, x2 - x6, x3 + x7, x3 - x7
    even, odd = a0 + a2, a1 + a3
    t, q = ROOT_HALF * (b1 - b3), ROOT_HALF * (b1 + b3)
    (e1r, e1i), (e3r, e3i) = half_sections(x0, x2, x4, x6)
    (o1r, o1i), (o3r, o3i) = half_sections(x1, x3, x5, x7)
    m1r, m1i = COS_EIGHTH * o1r + SIN_EIGHTH * o1i, COS_EIGHTH * o1i - SIN_EIGHTH * o1r
    m3r, m3i = SIN_EIGHTH * o3r + COS_EIGHTH * o3i, SIN_EIGHTH * o3i - COS_EIGHTH * o3r
    return [
        (even + odd, even - odd),
        (e1r + m1r, e1i + m1i),
        (b0 + t, -(b2 + q)),
        (e3r + m3r, e3i + m3i),
        (a0 - a2, a3 - a1),
        (e3r - m3r, m3i - e3i),
        (b0 - t, b2 - q),
        (e1r - m1r, m1i - e1i),
    ]


def half_gather(e1r, e1i, e3r, e3i):
    t, w = ROOT_HALF * (e1r - e3r), ROOT_HALF * (e1i + e3i)
    return e1r + e3r, t - w, e3i - e1i, -(t + w)


def gather_sections(v):
    (p0, p8), (p1, q1), (p2, q2), (p3, q3), (p4, q4), (p5, q5), (p6, q6), (p7, q7) = v
    even, odd = p0 + p8, p0 - p8
    a0, a2, a1, a3 = even + p4, even - p4, odd - q4, odd + q4
    b0, b2 = p2 + p6, q6 - q2
    t, w = ROOT_HALF * (p2 - p6), ROOT_HALF * (q2 + q6)
    b1, b3 = t - w, -(t + w)
    e1r, e1i, m1r, m1i = p1 + p7, q1 - q7, p1 - p7, q1 + q7
    e3r, e3i, m3r, m3i = p3 + p5, q3 - q5, p3 - p5, q3 + q5
    o1r, o1i = COS_EIGHTH * m1r - SIN_EIGHTH * m1i, SIN_EIGHTH * m1r + COS_EIGHTH * m1i
    o3r, o3i = SIN_EIGHTH * m3r - COS_EIGHTH * m3i, COS_EIGHTH * m3r + SIN_EIGHTH * m3i
    y0, y2, y4, y6 = half_gather(e1r, e1i, e3r, e3i)
    y1, y3, y5, y7 = half_gather(o1r, o1i, o3r, o3i)
    return [
        a0 + b0 + y0,
        a1 + b1 + y1,
        a2 + b2 + y2,
        a3 + b3 + y3,
        a0 - b0 + y4,
        a1 - b1 + y5,
        a2 - b2 + y6,
        a3 - b3 + y7,
    ]


def product_kernel(signal_ref, gate_ref, cotangent_ref, out_ref):
    for piece in range(out_ref.shape[0]):
        lanes = pl.ds(piece * INNER, INNER)
        out_ref[piece, 0] = signal_ref[0, :, lanes]
        out_ref[piece, 1] = (
            cotangent_ref[0, :, lanes].astype(F32) * gate_ref[0, :, lanes].astype(F32)
        ).astype(BF16)


def send_fields(signal, gate, cotangent, count):
    rows, width = signal.shape[1:]
    steps = 4
    field = pl.BlockSpec((1, rows, width // steps), lambda i: (0, 0, i))
    return pl.pallas_call(
        product_kernel,
        grid=(steps,),
        in_specs=[field] * 3,
        out_specs=pl.BlockSpec((count // steps, 2, rows, width // count), lambda i: (i, 0, 0, 0)),
        out_shape=jax.ShapeDtypeStruct((count, 2, rows, width // count), BF16),
        name="product",
    )(signal, gate, cotangent)


def taps_kernel(scale, taps_ref, table_ref, out_ref, sections_ref):
    @pl.when(pl.program_id(0) == 0)
    def _():
        def rows_step(i, _):
            start = pl.multiple_of(i * ROWS, ROWS)
            for lane in range(INNER // LANES):
                lanes = pl.ds(lane * LANES, LANES)
                x = [taps_ref[pl.ds(n * INNER + start, ROWS), lanes] * scale for n in range(8)]
                for j, (real, imag) in enumerate(sections(x)):
                    sections_ref[j, pl.ds(start, ROWS), lanes] = real.astype(BF16)
                    sections_ref[j, pl.ds(INNER + start, ROWS), lanes] = imag.astype(BF16)
            return 0

        lax.fori_loop(0, INNER // ROWS, rows_step, 0)

    out_ref[0] = jnp.dot(table_ref[0], sections_ref[pl.program_id(0)], preferred_element_type=F32)


def taps_spectrum(taps, forward):
    length, width = taps.shape
    table = pl.BlockSpec((1, 2 * INNER, 2 * INNER), lambda j: (j, 0, 0))
    return pl.pallas_call(
        functools.partial(taps_kernel, 1.0 / math.sqrt(length)),
        grid=(BLOCKS,),
        in_specs=[pl.BlockSpec((length, width), lambda j: (0, 0)), table],
        out_specs=pl.BlockSpec((1, 2 * INNER, width), lambda j: (j, 0, 0)),
        out_shape=jax.ShapeDtypeStruct((BLOCKS, 2 * INNER, width), F32),
        scratch_shapes=[pltpu.VMEM((BLOCKS, 2 * INNER, width), BF16)],
        compiler_params=pltpu.CompilerParams(vmem_limit_bytes=32 << 20),
        name="taps_spectrum",
    )(taps, forward)


def multiply_spectra(out_ref, slot, left_ref, right_ref, conjugate):
    real, imag = pl.ds(0, INNER), pl.ds(INNER, INNER)
    lr, li, rr, ri = left_ref[real, :], left_ref[imag, :], right_ref[real, :], right_ref[imag, :]
    if conjugate:
        pr, pi = lr * rr + li * ri, lr * ri - li * rr
    else:
        pr, pi = lr * rr - li * ri, lr * ri + li * rr
    out_ref[slot, real, :] = pr.astype(BF16)
    out_ref[slot, imag, :] = pi.astype(BF16)

    @pl.when(pl.program_id(0) == 0)
    def _():
        top, low = pl.ds(0, ROWS), pl.ds(INNER, ROWS)
        first = lax.broadcasted_iota(jnp.int32, (ROWS, INNER), 0) == 0
        alone_r, alone_i = left_ref[top, :] * right_ref[top, :], left_ref[low, :] * right_ref[low, :]
        out_ref[slot, top, :] = jnp.where(first, alone_r, pr[:ROWS]).astype(BF16)
        out_ref[slot, low, :] = jnp.where(first, alone_i, pi[:ROWS]).astype(BF16)


def transforms_kernel(
    scale,
    fields_ref,
    taps_ref,
    forward_ref,
    inverse_ref,
    back_ref,
    term_ref,
    sections_ref,
    signal_ref,
    product_ref,
    spectra_ref,
    parts_ref,
):
    step = pl.program_id(0)

    @pl.when(step == 0)
    def _():
        def rows_step(i, _):
            start = pl.multiple_of((i % 8) * ROWS, ROWS)
            place = pl.multiple_of(i * ROWS, ROWS)
            for field in range(2):
                for lane in range(INNER // LANES):
                    lanes = pl.ds(lane * LANES, LANES)
                    x = [
                        fields_ref[2 * n + i // 8, field, pl.ds(start, ROWS), lanes].astype(F32)
                        for n in range(8)
                    ]
                    for j, (real, imag) in enumerate(sections(x)):
                        sections_ref[field, j, pl.ds(place, ROWS), lanes] = real.astype(BF16)
                        sections_ref[field, j, pl.ds(INNER + place, ROWS), lanes] = imag.astype(BF16)
            return 0

        lax.fori_loop(0, INNER // ROWS, rows_step, 0)

    table, back_table = forward_ref[0], inverse_ref[0]
    signal_ref[...] = jnp.dot(table, sections_ref[0, step], preferred_element_type=F32)
    product_ref[...] = jnp.dot(table, sections_ref[1, step], preferred_element_type=F32)
    multiply_spectra(spectra_ref, 0, taps_ref.at[0], product_ref, True)
    multiply_spectra(spectra_ref, 1, taps_ref.at[0], signal_ref, False)
    multiply_spectra(spectra_ref, 2, signal_ref, product_ref, True)
    for out in range(3):
        parts_ref[out, step] = jnp.dot(back_table, spectra_ref[out], preferred_element_type=F32)

    @pl.when(step == BLOCKS - 1)
    def _():
        def rows_step(i, _):
            start = pl.multiple_of((i % 8) * ROWS, ROWS)
            place = pl.multiple_of(i * ROWS, ROWS)
            for out in range(3):
                for lane in range(INNER // LANES):
                    lanes = pl.ds(lane * LANES, LANES)
                    v = [
                        (
                            parts_ref[out, j, pl.ds(place, ROWS), lanes],
                            parts_ref[out, j, pl.ds(INNER + place, ROWS), lanes],
                        )
                        for j in range(BLOCKS)
                    ]
                    for n, y in enumerate(gather_sections(v)):
                        if out < 2:
                            back_ref[2 * n + i // 8, out, pl.ds(start, ROWS), lanes] = y.astype(BF16)
                        else:
                            term_ref[pl.ds(n * INNER + place, ROWS), lanes] = (y * scale).astype(BF16)
            return 0

        lax.fori_loop(0, INNER // ROWS, rows_step, 0)


def transforms(fields, taps_spec, forward, inverse):
    count, _, rows, width = fields.shape
    length = count * rows
    table = pl.BlockSpec((1, 2 * INNER, 2 * INNER), lambda j: (j, 0, 0))
    whole = pl.BlockSpec((count, 2, rows, width), lambda j: (0, 0, 0, 0))
    block = (2 * INNER, width)
    return pl.pallas_call(
        functools.partial(transforms_kernel, 1.0 / math.sqrt(length)),
        grid=(BLOCKS,),
        in_specs=[whole, pl.BlockSpec((1,) + block, lambda j: (j, 0, 0)), table, table],
        out_specs=[whole, pl.BlockSpec((length, width), lambda j: (0, 0))],
        out_shape=[
            jax.ShapeDtypeStruct(fields.shape, BF16),
            jax.ShapeDtypeStruct((length, width), BF16),
        ],
        scratch_shapes=[
            pltpu.VMEM((2, BLOCKS) + block, BF16),
            pltpu.VMEM(block, F32),
            pltpu.VMEM(block, F32),
            pltpu.VMEM((3,) + block, BF16),
            pltpu.VMEM((3, BLOCKS) + block, F32),
        ],
        compiler_params=pltpu.CompilerParams(vmem_limit_bytes=48 << 20),
        name="transforms",
    )(fields, taps_spec, forward, inverse)


def outputs_kernel(back_ref, cotangent_ref, signal_grad_ref, gate_grad_ref):
    for piece in range(back_ref.shape[0]):
        lanes = pl.ds(piece * INNER, INNER)
        signal_grad_ref[0, :, lanes] = back_ref[piece, 0]
        gate_grad_ref[0, :, lanes] = (
            cotangent_ref[0, :, lanes].astype(F32) * back_ref[piece, 1].astype(F32)
        ).astype(BF16)


def place_outputs(back, cotangent):
    count, _, rows, width = back.shape
    steps = 4
    field = pl.BlockSpec((1, rows, cotangent.shape[2] // steps), lambda i: (0, 0, i))
    return pl.pallas_call(
        outputs_kernel,
        grid=(steps,),
        in_specs=[
            pl.BlockSpec((count // steps, 2, rows, width), lambda i: (i, 0, 0, 0)),
            field,
        ],
        out_specs=[field, field],
        out_shape=[jax.ShapeDtypeStruct(cotangent.shape, BF16)] * 2,
        name="outputs",
    )(back, cotangent)


def exchange(term, mine, pairs):
    keep = lax.dynamic_index_in_dim(term, mine, 0, keepdims=False)
    away = lax.dynamic_index_in_dim(term, 1 - mine, 0, keepdims=False).astype(BF16)
    return keep.astype(F32) + lax.ppermute(away, "dp", pairs).astype(F32)


def sum_over_sequences(term):
    devices = lax.axis_size("dp")
    index = lax.axis_index("dp")
    width = term.shape[1]
    share = term.shape[0] // devices
    y_pairs = [(d, ((3 - d // 2) * 2) + d % 2) for d in range(devices)]
    total = exchange(term.reshape(2, devices // 2, share, width), index // 4, y_pairs)
    total = exchange(total.reshape(2, devices // 4, share, width), (index // 2) % 2, [(d, d ^ 2) for d in range(devices)])
    return exchange(total.reshape(2, share, width), index % 2, [(d, d ^ 1) for d in range(devices)])


def local(signal, gate, cotangent, filter_taps):
    count = lax.axis_size("ctx")
    forward, inverse = section_tables()
    fields = lax.all_to_all(send_fields(signal, gate, cotangent, count), "ctx", 0, 0, tiled=True)
    taps_spec = taps_spectrum(filter_taps, forward)
    back, term = transforms(fields, taps_spec, forward, inverse)
    back = lax.all_to_all(back, "ctx", 0, 0, tiled=True)
    taps_grad = sum_over_sequences(term)
    signal_grad, gate_grad = place_outputs(back, cotangent)
    return (signal_grad, gate_grad, taps_grad)


def solution(mesh):
    in_specs = (P("dp", "ctx", None), P("dp", "ctx", None), P("dp", "ctx", None), P(None, "ctx"))
    out_specs = (P("dp", "ctx", None), P("dp", "ctx", None), P("dp", "ctx"))
    return jax.shard_map(local, mesh=mesh, in_specs=in_specs, out_specs=out_specs, check_vma=False)
```

```python
import functools
import math

import jax
import jax.numpy as jnp
import ml_dtypes
import numpy as np
from jax import lax
from jax.experimental import pallas as pl
from jax.experimental.pallas import tpu as pltpu
from jax.sharding import PartitionSpec as P

F32 = jnp.float32
BF16 = jnp.bfloat16
RADIX = 32
INNER = 128
TOTAL = RADIX * INNER
BLOCKS = RADIX // 2
ROOT_HALF = math.sqrt(0.5)
COS_EIGHTH = math.cos(math.pi / 8)
SIN_EIGHTH = math.sin(math.pi / 8)
TURNS = [(math.cos(math.pi * k / 16), math.sin(math.pi * k / 16)) for k in (1, 3, 5, 7)]
CHANNELS = 256
ROWS = 16
LANES = 128


def section_tables():
    column = np.arange(INNER)[None, :]
    forward = np.zeros((BLOCKS, 2 * INNER, 2 * INNER))
    half = INNER // 2
    row = np.arange(half)[:, None]
    for section in range(2):
        angle = 2 * np.pi * ((column * (RADIX * row + BLOCKS * section)) % TOTAL) / TOTAL
        place = slice(section * INNER, (section + 1) * INNER)
        forward[0, section * half : (section + 1) * half, place] = np.cos(angle)
        forward[0, INNER + section * half : INNER + (section + 1) * half, place] = -np.sin(angle)
    forward[0, INNER, :INNER] = np.cos(np.pi * column[0])
    row = np.arange(INNER)[:, None]
    for j in range(1, BLOCKS):
        angle = 2 * np.pi * ((column * (RADIX * row + j)) % TOTAL) / TOTAL
        forward[j] = np.block([[np.cos(angle), np.sin(angle)], [-np.sin(angle), np.cos(angle)]])
    return forward.astype(ml_dtypes.bfloat16)


def half_sections(y0, y2, y4, y6):
    t, q = ROOT_HALF * (y2 - y6), ROOT_HALF * (y2 + y6)
    return (y0 + t, -(y4 + q)), (y0 - t, y4 - q)


def odd_sections(x):
    x0, x1, x2, x3, x4, x5, x6, x7 = x
    (e1r, e1i), (e3r, e3i) = half_sections(x0, x2, x4, x6)
    (o1r, o1i), (o3r, o3i) = half_sections(x1, x3, x5, x7)
    m1r, m1i = COS_EIGHTH * o1r + SIN_EIGHTH * o1i, COS_EIGHTH * o1i - SIN_EIGHTH * o1r
    m3r, m3i = SIN_EIGHTH * o3r + COS_EIGHTH * o3i, SIN_EIGHTH * o3i - COS_EIGHTH * o3r
    return (e1r + m1r, e1i + m1i), (e3r + m3r, e3i + m3i), (e3r - m3r, m3i - e3i), (e1r - m1r, m1i - e1i)


def sections(x):
    a = [x[n] + x[n + 8] for n in range(8)]
    b = [x[n] - x[n + 8] for n in range(8)]
    c = [a[n] + a[n + 4] for n in range(4)]
    d = [a[n] - a[n + 4] for n in range(4)]
    even, odd = c[0] + c[2], c[1] + c[3]
    t, q = ROOT_HALF * (d[1] - d[3]), ROOT_HALF * (d[1] + d[3])
    out = [None] * 16
    out[0] = (even + odd, even - odd)
    out[4] = (d[0] + t, -(d[2] + q))
    out[8] = (c[0] - c[2], c[3] - c[1])
    out[12] = (d[0] - t, d[2] - q)
    out[2], out[6], out[10], out[14] = odd_sections(b)
    pairs = zip((1, 3, 5, 7), TURNS, odd_sections(x[0::2]), odd_sections(x[1::2]))
    for k, (cos, sin), (er, ei), (tr, ti) in pairs:
        mr, mi = cos * tr + sin * ti, cos * ti - sin * tr
        out[k] = (er + mr, ei + mi)
        out[16 - k] = (er - mr, mi - ei)
    return out


def half_gather(e1r, e1i, e3r, e3i):
    t, w = ROOT_HALF * (e1r - e3r), ROOT_HALF * (e1i + e3i)
    return e1r + e3r, t - w, e3i - e1i, -(t + w)


def odd_gather(v1, v3, v5, v7):
    e1r, e1i, m1r, m1i = v1[0] + v7[0], v1[1] - v7[1], v1[0] - v7[0], v1[1] + v7[1]
    e3r, e3i, m3r, m3i = v3[0] + v5[0], v3[1] - v5[1], v3[0] - v5[0], v3[1] + v5[1]
    o1r, o1i = COS_EIGHTH * m1r - SIN_EIGHTH * m1i, SIN_EIGHTH * m1r + COS_EIGHTH * m1i
    o3r, o3i = SIN_EIGHTH * m3r - COS_EIGHTH * m3i, COS_EIGHTH * m3r + SIN_EIGHTH * m3i
    y0, y2, y4, y6 = half_gather(e1r, e1i, e3r, e3i)
    y1, y3, y5, y7 = half_gather(o1r, o1i, o3r, o3i)
    return [y0, y1, y2, y3, y4, y5, y6, y7]


def gather_sections(v):
    even, odd = v[0][0] + v[0][1], v[0][0] - v[0][1]
    c = [even + v[8][0], odd - v[8][1], even - v[8][0], odd + v[8][1]]
    t, w = ROOT_HALF * (v[4][0] - v[12][0]), ROOT_HALF * (v[4][1] + v[12][1])
    d = [v[4][0] + v[12][0], t - w, v[12][1] - v[4][1], -(t + w)]
    a = [c[n] + d[n] for n in range(4)] + [c[n] - d[n] for n in range(4)]
    b = odd_gather(v[2], v[6], v[10], v[14])
    straight, turned = [], []
    for k, (cos, sin) in zip((1, 3, 5, 7), TURNS):
        (pr, pi), (qr, qi) = v[k], v[16 - k]
        mr, mi = pr - qr, pi + qi
        straight.append((pr + qr, pi - qi))
        turned.append((cos * mr - sin * mi, sin * mr + cos * mi))
    ye, yo = odd_gather(*straight), odd_gather(*turned)
    y = [part for both in zip(ye, yo) for part in both]
    return [a[n] + b[n] + y[n] for n in range(8)] + [a[n] - b[n] + y[n + 8] for n in range(8)]


HBM = pl.BlockSpec(memory_space=pltpu.HBM)
VMEM = pl.BlockSpec(memory_space=pltpu.VMEM)
PARTS = 4


def product_kernel(signal_ref, gate_ref, cotangent_ref, out_ref, fields, products, in_sems, out_sems):
    each = fields.shape[2] // PARTS
    pieces = each // CHANNELS
    loads = []
    for part in range(PARTS):
        lanes = pl.ds(part * each, each)
        for field, ref in enumerate((gate_ref, cotangent_ref, signal_ref)):
            loads.append(pltpu.make_async_copy(ref.at[0, :, lanes], fields.at[field, :, lanes], in_sems.at[part, field]))
            loads[-1].start()
    stores = []
    for part in range(PARTS):
        for field in range(2):
            loads[3 * part + field].wait()
        for piece in range(part * pieces, (part + 1) * pieces):
            lanes = pl.ds(piece * CHANNELS, CHANNELS)
            products[piece] = (fields[1, :, lanes].astype(F32) * fields[0, :, lanes].astype(F32)).astype(BF16)
        whole = pl.ds(part * pieces, pieces)
        stores.append(pltpu.make_async_copy(products.at[whole], out_ref.at[whole, 1], out_sems.at[part]))
        stores[-1].start()
        loads[3 * part + 2].wait()
        for piece in range(part * pieces, (part + 1) * pieces):
            lanes = pl.ds(piece * CHANNELS, CHANNELS)
            stores.append(pltpu.make_async_copy(fields.at[2, :, lanes], out_ref.at[piece, 0], out_sems.at[PARTS + piece]))
            stores[-1].start()
    for store in stores:
        store.wait()


def send_fields(signal, gate, cotangent, count):
    rows, width = signal.shape[1:]
    return pl.pallas_call(
        product_kernel,
        in_specs=[HBM] * 3,
        out_specs=HBM,
        out_shape=jax.ShapeDtypeStruct((count, 2, rows, width // count), BF16),
        scratch_shapes=[
            pltpu.VMEM((3, rows, width), BF16),
            pltpu.VMEM((count, rows, width // count), BF16),
            pltpu.SemaphoreType.DMA((PARTS, 3)),
            pltpu.SemaphoreType.DMA((PARTS + count,)),
        ],
        compiler_params=pltpu.CompilerParams(vmem_limit_bytes=60 << 20),
        name="product",
    )(signal, gate, cotangent)


def chunk_of(i):
    start = pl.multiple_of((i // 2) * ROWS, ROWS)
    lanes = pl.ds(pl.multiple_of((i % 2) * LANES, LANES), LANES)
    return pl.ds(start, ROWS), pl.ds(pl.multiple_of(INNER + start, ROWS), ROWS), lanes


def split_chunk(i, sections_ref, load):
    rows, low, lanes = chunk_of(i)
    x = [load(n, rows, lanes) for n in range(RADIX // 2)]
    for j, (real, imag) in enumerate(sections(x)):
        sections_ref[j, rows, lanes] = real.astype(BF16)
        sections_ref[j, low, lanes] = imag.astype(BF16)


def gather_chunk(i, parts_ref, store):
    rows, low, lanes = chunk_of(i)
    v = [(parts_ref[j, rows, lanes], parts_ref[j, low, lanes]) for j in range(BLOCKS)]
    for n, y in enumerate(gather_sections(v)):
        store(n, rows, lanes, y)


def repeat(step):
    def body(i, _):
        step(i)
        return 0

    lax.fori_loop(0, BLOCKS, body, 0, unroll=True)


def taps_kernel(scale, taps_ref, forward_ref, out_ref, sections_ref):
    def load(n, rows, lanes):
        return taps_ref[pl.ds(pl.multiple_of(n * INNER + rows.start, ROWS), ROWS), lanes] * scale

    repeat(lambda i: split_chunk(i, sections_ref, load))
    for j in range(BLOCKS):
        out_ref[j] = jnp.dot(forward_ref[j], sections_ref[j], preferred_element_type=F32).astype(BF16)


def taps_spectrum(taps, forward):
    length, width = taps.shape
    return pl.pallas_call(
        functools.partial(taps_kernel, 2.0 / TOTAL / math.sqrt(length)),
        in_specs=[VMEM, VMEM],
        out_specs=VMEM,
        out_shape=jax.ShapeDtypeStruct((BLOCKS, 2 * INNER, width), BF16),
        scratch_shapes=[pltpu.VMEM((BLOCKS, 2 * INNER, width), BF16)],
        compiler_params=pltpu.CompilerParams(vmem_limit_bytes=24 << 20),
        name="taps_spectrum",
    )(taps, forward)


def multiply_spectra(left, right, conjugate, lone):
    lr, li, rr, ri = left[:INNER], left[INNER:], right[:INNER], right[INNER:]
    if conjugate:
        pr, pi = lr * rr + li * ri, lr * ri - li * rr
    else:
        pr, pi = lr * rr - li * ri, lr * ri + li * rr
    if lone:
        first = lax.broadcasted_iota(jnp.int32, pr.shape, 0) == 0
        pr, pi = jnp.where(first, 0.5 * lr * rr, pr), jnp.where(first, 0.5 * li * ri, pi)
    return jnp.concatenate([pr.astype(BF16), pi.astype(BF16)], axis=0)


def transforms_kernel(
    scale,
    fields_hbm,
    taps_hbm,
    forward_hbm,
    back_ref,
    term_0_ref,
    term_1_ref,
    term_2_ref,
    term_3_ref,
    fields_ref,
    taps_ref,
    forward_ref,
    sections_ref,
    signal_ref,
    spectra_ref,
    parts_ref,
    back_buf,
    term_buf,
    load_sems,
    store_sems,
):
    loads = []

    def load(hbm, vmem, pieces):
        each = hbm.shape[0] // pieces
        for piece in range(pieces):
            part = pl.ds(piece * each, each)
            loads.append(pltpu.make_async_copy(hbm.at[part], vmem.at[part], load_sems.at[len(loads)]))
            loads[-1].start()
        return loads[-pieces:]

    def finish(copies):
        for copy in copies:
            copy.wait()

    stores = []

    def store_copy(source, target):
        stores.append(pltpu.make_async_copy(source, target, store_sems.at[len(stores)]))
        stores[-1].start()

    def split(i, field):
        split_chunk(
            i, sections_ref.at[field], lambda n, rows, lanes: fields_ref[field, n, rows, lanes].astype(F32)
        )

    def gather(i, out):
        def store(n, rows, lanes, y):
            if out == 2:
                place = pl.ds(pl.multiple_of((n % 2) * INNER + rows.start, ROWS), ROWS)
                term_buf[n // 4, (n // 2) % 2, place, lanes] = (y * scale).astype(BF16)
            else:
                back_buf[out, n, rows, lanes] = y.astype(BF16)

        gather_chunk(i, parts_ref.at[out], store)

    def forward(j, field):
        return jnp.dot(forward_ref[j], sections_ref[field, j], preferred_element_type=F32)

    def inverse(j, out):
        parts_ref[out, j] = lax.dot_general(
            forward_ref[j], spectra_ref[out, j], (((0,), (0,)), ((), ())), preferred_element_type=F32
        )

    def multiply(j, lone):
        product, taps, signal = forward(j, 1), taps_ref[j].astype(F32), signal_ref[j]
        spectra_ref[0, j] = multiply_spectra(taps, product, True, lone)
        spectra_ref[1, j] = multiply_spectra(taps, signal, False, lone)
        spectra_ref[2, j] = multiply_spectra(signal, product, True, lone)

    def second_split(i):
        split(i, 1)
        signal_ref[i] = forward(i, 0)

    def first_gather(i):
        gather(i, 2)
        inverse(i, 0)

    def second_gather(i):
        gather(i, 0)
        inverse(i, 1)

    first_load = load(fields_hbm.at[:, 0], fields_ref.at[0], 4)
    second_load = load(fields_hbm.at[:, 1], fields_ref.at[1], 2)
    forward_load = load(forward_hbm, forward_ref, 2)
    taps_load = load(taps_hbm, taps_ref, 2)
    finish(first_load)
    repeat(lambda i: split(i, 0))
    finish(forward_load + second_load)
    repeat(second_split)
    finish(taps_load)
    for j in range(BLOCKS):
        multiply(j, j == 0)
    repeat(lambda i: inverse(i, 2))
    repeat(first_gather)
    column, side = lax.axis_index("dp") // 2, lax.axis_index("dp") % 2
    for turn, ref in enumerate((term_0_ref, term_1_ref, term_2_ref, term_3_ref)):
        for half in range(2):
            store_copy(term_buf.at[(column + turn) % 4, (side + half) % 2], ref.at[half])
    repeat(second_gather)
    store_copy(back_buf.at[0], back_ref.at[:, 0])
    for quarter in range(4):
        for i in range(quarter * 4, quarter * 4 + 4):
            gather(i, 1)
        rows = pl.ds(quarter * 2 * ROWS, 2 * ROWS)
        store_copy(back_buf.at[1, :, rows], back_ref.at[:, 1, rows])
    finish(stores)


def transforms(fields, taps_spec, forward):
    count, _, rows, width = fields.shape
    length = count * rows
    block = (2 * INNER, width)
    return pl.pallas_call(
        functools.partial(transforms_kernel, 2.0 / TOTAL / math.sqrt(length)),
        in_specs=[HBM] * 3,
        out_specs=[HBM] * 5,
        out_shape=[jax.ShapeDtypeStruct(fields.shape, BF16)]
        + [jax.ShapeDtypeStruct((2, length // 8, width), BF16)] * 4,
        scratch_shapes=[
            pltpu.VMEM((2, count, rows, width), BF16),
            pltpu.VMEM((BLOCKS,) + block, BF16),
            pltpu.VMEM(forward.shape, BF16),
            pltpu.VMEM((2, BLOCKS) + block, BF16),
            pltpu.VMEM((BLOCKS,) + block, F32),
            pltpu.VMEM((3, BLOCKS) + block, BF16),
            pltpu.VMEM((3, BLOCKS) + block, F32),
            pltpu.VMEM((2, count, rows, width), BF16),
            pltpu.VMEM((4, 2, length // 8, width), BF16),
            pltpu.SemaphoreType.DMA((16,)),
            pltpu.SemaphoreType.DMA((13,)),
        ],
        compiler_params=pltpu.CompilerParams(vmem_limit_bytes=61 << 20),
        name="transforms",
    )(fields, taps_spec, forward)


def outputs_kernel(back_ref, cotangent_ref, signal_grad_ref, gate_grad_ref, gate_buf, sems):
    count = back_ref.shape[0]
    pieces = count // PARTS
    stores = []
    for piece in range(count):
        lanes = pl.ds(piece * CHANNELS, CHANNELS)
        stores.append(pltpu.make_async_copy(back_ref.at[piece, 0], signal_grad_ref.at[0, :, lanes], sems.at[piece]))
        stores[-1].start()
    for part in range(PARTS):
        for piece in range(part * pieces, (part + 1) * pieces):
            lanes = pl.ds(piece * CHANNELS, CHANNELS)
            gate_buf[:, lanes] = (cotangent_ref[0, :, lanes].astype(F32) * back_ref[piece, 1].astype(F32)).astype(BF16)
        lanes = pl.ds(part * pieces * CHANNELS, pieces * CHANNELS)
        stores.append(pltpu.make_async_copy(gate_buf.at[:, lanes], gate_grad_ref.at[0, :, lanes], sems.at[count + part]))
        stores[-1].start()
    for store in stores:
        store.wait()


def place_outputs(back, cotangent):
    return pl.pallas_call(
        outputs_kernel,
        in_specs=[VMEM, VMEM],
        out_specs=[HBM, HBM],
        out_shape=[jax.ShapeDtypeStruct(cotangent.shape, BF16)] * 2,
        scratch_shapes=[
            pltpu.VMEM(cotangent.shape[1:], BF16),
            pltpu.SemaphoreType.DMA((back.shape[0] + PARTS,)),
        ],
        compiler_params=pltpu.CompilerParams(vmem_limit_bytes=12 << 20),
        name="outputs",
    )(back, cotangent)


def sum_over_sequences(quarters):
    devices = lax.axis_size("dp")
    terms = [quarters[0]]
    for turn in (2, 1, 3):
        terms.append(lax.ppermute(quarters[turn], "dp", [(d, (d + 2 * turn) % devices) for d in range(devices)]))
    keep, away = (sum(term[half].astype(F32) for term in terms) for half in range(2))
    return keep, lax.ppermute(away.astype(BF16), "dp", [(d, d ^ 1) for d in range(devices)])


def local(signal, gate, cotangent, filter_taps):
    count = lax.axis_size("ctx")
    forward = section_tables()
    fields = lax.all_to_all(send_fields(signal, gate, cotangent, count), "ctx", 0, 0, tiled=True)
    taps_spec = taps_spectrum(filter_taps, forward)
    back, *quarters = transforms(fields, taps_spec, forward)
    back = lax.all_to_all(back, "ctx", 0, 0, tiled=True)
    keep, other = sum_over_sequences(quarters)
    signal_grad, gate_grad = place_outputs(back, cotangent)
    signal_grad, other = lax.optimization_barrier((signal_grad, other))
    return (signal_grad, gate_grad, keep + other.astype(F32))


def solution(mesh):
    in_specs = (P("dp", "ctx", None), P("dp", "ctx", None), P("dp", "ctx", None), P(None, "ctx"))
    out_specs = (P("dp", "ctx", None), P("dp", "ctx", None), P("dp", "ctx"))
    return jax.shard_map(local, mesh=mesh, in_specs=in_specs, out_specs=out_specs, check_vma=False)
```

```python
import functools
import math

import jax
import jax.numpy as jnp
import ml_dtypes
import numpy as np
from jax import lax
from jax.experimental import pallas as pl
from jax.experimental.pallas import tpu as pltpu
from jax.sharding import PartitionSpec as P

F32 = jnp.float32
BF16 = jnp.bfloat16
RADIX = 32
INNER = 128
TOTAL = RADIX * INNER
BLOCKS = RADIX // 2
ROOT_HALF = math.sqrt(0.5)
COS_EIGHTH = math.cos(math.pi / 8)
SIN_EIGHTH = math.sin(math.pi / 8)
TURNS = [(math.cos(math.pi * k / 16), math.sin(math.pi * k / 16)) for k in (1, 3, 5, 7)]
CHANNELS = 256
ROWS = 16
LANES = 128


def section_tables():
    column = np.arange(INNER)[None, :]
    forward = np.zeros((BLOCKS, 2 * INNER, 2 * INNER))
    half = INNER // 2
    row = np.arange(half)[:, None]
    for section in range(2):
        angle = 2 * np.pi * ((column * (RADIX * row + BLOCKS * section)) % TOTAL) / TOTAL
        place = slice(section * INNER, (section + 1) * INNER)
        forward[0, section * half : (section + 1) * half, place] = np.cos(angle)
        forward[0, INNER + section * half : INNER + (section + 1) * half, place] = -np.sin(angle)
    forward[0, INNER, :INNER] = np.cos(np.pi * column[0])
    row = np.arange(INNER)[:, None]
    for j in range(1, BLOCKS):
        angle = 2 * np.pi * ((column * (RADIX * row + j)) % TOTAL) / TOTAL
        forward[j] = np.block([[np.cos(angle), np.sin(angle)], [-np.sin(angle), np.cos(angle)]])
    return forward.astype(ml_dtypes.bfloat16)


def half_sections(y0, y2, y4, y6):
    t, q = ROOT_HALF * (y2 - y6), ROOT_HALF * (y2 + y6)
    return (y0 + t, -(y4 + q)), (y0 - t, y4 - q)


def odd_sections(x):
    x0, x1, x2, x3, x4, x5, x6, x7 = x
    (e1r, e1i), (e3r, e3i) = half_sections(x0, x2, x4, x6)
    (o1r, o1i), (o3r, o3i) = half_sections(x1, x3, x5, x7)
    m1r, m1i = COS_EIGHTH * o1r + SIN_EIGHTH * o1i, COS_EIGHTH * o1i - SIN_EIGHTH * o1r
    m3r, m3i = SIN_EIGHTH * o3r + COS_EIGHTH * o3i, SIN_EIGHTH * o3i - COS_EIGHTH * o3r
    return (e1r + m1r, e1i + m1i), (e3r + m3r, e3i + m3i), (e3r - m3r, m3i - e3i), (e1r - m1r, m1i - e1i)


def sections(x):
    a = [x[n] + x[n + 8] for n in range(8)]
    b = [x[n] - x[n + 8] for n in range(8)]
    c = [a[n] + a[n + 4] for n in range(4)]
    d = [a[n] - a[n + 4] for n in range(4)]
    even, odd = c[0] + c[2], c[1] + c[3]
    t, q = ROOT_HALF * (d[1] - d[3]), ROOT_HALF * (d[1] + d[3])
    out = [None] * 16
    out[0] = (even + odd, even - odd)
    out[4] = (d[0] + t, -(d[2] + q))
    out[8] = (c[0] - c[2], c[3] - c[1])
    out[12] = (d[0] - t, d[2] - q)
    out[2], out[6], out[10], out[14] = odd_sections(b)
    pairs = zip((1, 3, 5, 7), TURNS, odd_sections(x[0::2]), odd_sections(x[1::2]))
    for k, (cos, sin), (er, ei), (tr, ti) in pairs:
        mr, mi = cos * tr + sin * ti, cos * ti - sin * tr
        out[k] = (er + mr, ei + mi)
        out[16 - k] = (er - mr, mi - ei)
    return out


def half_gather(e1r, e1i, e3r, e3i):
    t, w = ROOT_HALF * (e1r - e3r), ROOT_HALF * (e1i + e3i)
    return e1r + e3r, t - w, e3i - e1i, -(t + w)


def odd_gather(v1, v3, v5, v7):
    e1r, e1i, m1r, m1i = v1[0] + v7[0], v1[1] - v7[1], v1[0] - v7[0], v1[1] + v7[1]
    e3r, e3i, m3r, m3i = v3[0] + v5[0], v3[1] - v5[1], v3[0] - v5[0], v3[1] + v5[1]
    o1r, o1i = COS_EIGHTH * m1r - SIN_EIGHTH * m1i, SIN_EIGHTH * m1r + COS_EIGHTH * m1i
    o3r, o3i = SIN_EIGHTH * m3r - COS_EIGHTH * m3i, COS_EIGHTH * m3r + SIN_EIGHTH * m3i
    y0, y2, y4, y6 = half_gather(e1r, e1i, e3r, e3i)
    y1, y3, y5, y7 = half_gather(o1r, o1i, o3r, o3i)
    return [y0, y1, y2, y3, y4, y5, y6, y7]


def gather_sections(v):
    even, odd = v[0][0] + v[0][1], v[0][0] - v[0][1]
    c = [even + v[8][0], odd - v[8][1], even - v[8][0], odd + v[8][1]]
    t, w = ROOT_HALF * (v[4][0] - v[12][0]), ROOT_HALF * (v[4][1] + v[12][1])
    d = [v[4][0] + v[12][0], t - w, v[12][1] - v[4][1], -(t + w)]
    a = [c[n] + d[n] for n in range(4)] + [c[n] - d[n] for n in range(4)]
    b = odd_gather(v[2], v[6], v[10], v[14])
    straight, turned = [], []
    for k, (cos, sin) in zip((1, 3, 5, 7), TURNS):
        (pr, pi), (qr, qi) = v[k], v[16 - k]
        mr, mi = pr - qr, pi + qi
        straight.append((pr + qr, pi - qi))
        turned.append((cos * mr - sin * mi, sin * mr + cos * mi))
    ye, yo = odd_gather(*straight), odd_gather(*turned)
    y = [part for both in zip(ye, yo) for part in both]
    return [a[n] + b[n] + y[n] for n in range(8)] + [a[n] - b[n] + y[n + 8] for n in range(8)]


HBM = pl.BlockSpec(memory_space=pltpu.HBM)
VMEM = pl.BlockSpec(memory_space=pltpu.VMEM)
PARTS = 4


def product_kernel(signal_ref, gate_ref, cotangent_ref, out_ref, fields, products, in_sems, out_sems):
    each = fields.shape[2] // PARTS
    pieces = each // CHANNELS
    loads = []
    for part in range(PARTS):
        lanes = pl.ds(part * each, each)
        for field, ref in enumerate((gate_ref, cotangent_ref, signal_ref)):
            loads.append(pltpu.make_async_copy(ref.at[0, :, lanes], fields.at[field, :, lanes], in_sems.at[part, field]))
            loads[-1].start()
    stores = []
    for part in range(PARTS):
        for field in range(2):
            loads[3 * part + field].wait()
        for piece in range(part * pieces, (part + 1) * pieces):
            lanes = pl.ds(piece * CHANNELS, CHANNELS)
            products[piece] = (fields[1, :, lanes].astype(F32) * fields[0, :, lanes].astype(F32)).astype(BF16)
        whole = pl.ds(part * pieces, pieces)
        stores.append(pltpu.make_async_copy(products.at[whole], out_ref.at[whole, 1], out_sems.at[part]))
        stores[-1].start()
        loads[3 * part + 2].wait()
        for piece in range(part * pieces, (part + 1) * pieces):
            lanes = pl.ds(piece * CHANNELS, CHANNELS)
            stores.append(pltpu.make_async_copy(fields.at[2, :, lanes], out_ref.at[piece, 0], out_sems.at[PARTS + piece]))
            stores[-1].start()
    for store in stores:
        store.wait()


def send_fields(signal, gate, cotangent, count):
    rows, width = signal.shape[1:]
    return pl.pallas_call(
        product_kernel,
        in_specs=[HBM] * 3,
        out_specs=HBM,
        out_shape=jax.ShapeDtypeStruct((count, 2, rows, width // count), BF16),
        scratch_shapes=[
            pltpu.VMEM((3, rows, width), BF16),
            pltpu.VMEM((count, rows, width // count), BF16),
            pltpu.SemaphoreType.DMA((PARTS, 3)),
            pltpu.SemaphoreType.DMA((PARTS + count,)),
        ],
        compiler_params=pltpu.CompilerParams(vmem_limit_bytes=60 << 20),
        name="product",
    )(signal, gate, cotangent)


def chunk_of(i):
    start = pl.multiple_of((i // 2) * ROWS, ROWS)
    lanes = pl.ds(pl.multiple_of((i % 2) * LANES, LANES), LANES)
    return pl.ds(start, ROWS), pl.ds(pl.multiple_of(INNER + start, ROWS), ROWS), lanes


def split_chunk(i, sections_ref, load):
    rows, low, lanes = chunk_of(i)
    x = [load(n, rows, lanes) for n in range(RADIX // 2)]
    for j, (real, imag) in enumerate(sections(x)):
        sections_ref[j, rows, lanes] = real.astype(BF16)
        sections_ref[j, low, lanes] = imag.astype(BF16)


def gather_chunk(i, parts_ref, store):
    rows, low, lanes = chunk_of(i)
    v = [(parts_ref[j, rows, lanes], parts_ref[j, low, lanes]) for j in range(BLOCKS)]
    for n, y in enumerate(gather_sections(v)):
        store(n, rows, lanes, y)


def repeat(step):
    def body(i, _):
        step(i)
        return 0

    lax.fori_loop(0, BLOCKS, body, 0, unroll=True)


def taps_kernel(scale, taps_ref, forward_ref, out_ref, sections_ref):
    def load(n, rows, lanes):
        return taps_ref[pl.ds(pl.multiple_of(n * INNER + rows.start, ROWS), ROWS), lanes] * scale

    repeat(lambda i: split_chunk(i, sections_ref, load))
    for j in range(BLOCKS):
        out_ref[j] = jnp.dot(forward_ref[j], sections_ref[j], preferred_element_type=F32).astype(BF16)


def taps_spectrum(taps, forward):
    length, width = taps.shape
    return pl.pallas_call(
        functools.partial(taps_kernel, 2.0 / TOTAL / math.sqrt(length)),
        in_specs=[VMEM, VMEM],
        out_specs=VMEM,
        out_shape=jax.ShapeDtypeStruct((BLOCKS, 2 * INNER, width), BF16),
        scratch_shapes=[pltpu.VMEM((BLOCKS, 2 * INNER, width), BF16)],
        compiler_params=pltpu.CompilerParams(vmem_limit_bytes=24 << 20),
        name="taps_spectrum",
    )(taps, forward)


def multiply_spectra(left, right, conjugate, lone):
    lr, li, rr, ri = left[:INNER], left[INNER:], right[:INNER], right[INNER:]
    if conjugate:
        pr, pi = lr * rr + li * ri, lr * ri - li * rr
    else:
        pr, pi = lr * rr - li * ri, lr * ri + li * rr
    if lone:
        first = lax.broadcasted_iota(jnp.int32, pr.shape, 0) == 0
        pr, pi = jnp.where(first, 0.5 * lr * rr, pr), jnp.where(first, 0.5 * li * ri, pi)
    return jnp.concatenate([pr.astype(BF16), pi.astype(BF16)], axis=0)


class Copies:
    def __init__(self, sems):
        self.sems, self.used = sems, 0

    def start(self, source, target, pieces=1):
        each = source.shape[0] // pieces
        copies = []
        for piece in range(pieces):
            part = pl.ds(piece * each, each)
            copies.append(pltpu.make_async_copy(source.at[part], target.at[part], self.sems.at[self.used]))
            copies[-1].start()
            self.used += 1
        return copies


def finish(copies):
    for copy in copies:
        copy.wait()


def backward(table, spectrum):
    return lax.dot_general(table, spectrum, (((0,), (0,)), ((), ())), preferred_element_type=F32)


def transforms_kernel(
    fields_hbm,
    taps_hbm,
    forward_hbm,
    back_ref,
    cross_ref,
    fields_ref,
    taps_ref,
    forward_ref,
    sections_ref,
    signal_ref,
    spectra_ref,
    cross_buf,
    parts_ref,
    back_buf,
    sems,
):
    copies = Copies(sems)
    first_load = copies.start(fields_hbm.at[:, 0], fields_ref.at[0], 4)
    second_load = copies.start(fields_hbm.at[:, 1], fields_ref.at[1], 2)
    forward_load = copies.start(forward_hbm, forward_ref, 2)
    taps_load = copies.start(taps_hbm, taps_ref, 2)
    stores = []

    def split(i, field):
        split_chunk(
            i, sections_ref.at[field], lambda n, rows, lanes: fields_ref[field, n, rows, lanes].astype(F32)
        )

    def gather(i, out):
        def store(n, rows, lanes, y):
            back_buf[out, n, rows, lanes] = y.astype(BF16)

        gather_chunk(i, parts_ref.at[out], store)

    def forward(j, field):
        return jnp.dot(forward_ref[j], sections_ref[field, j], preferred_element_type=F32)

    def inverse(j, out):
        parts_ref[out, j] = backward(forward_ref[j], spectra_ref[out, j])

    def multiply(j, lone):
        product, taps, signal = forward(j, 1), taps_ref[j].astype(F32), signal_ref[j]
        cross_buf[j] = multiply_spectra(signal, product, True, lone)
        spectra_ref[0, j] = multiply_spectra(taps, product, True, lone)
        spectra_ref[1, j] = multiply_spectra(taps, signal, False, lone)

    def second_split(i):
        split(i, 1)
        signal_ref[i] = forward(i, 0)

    def first_gather(i):
        gather(i, 0)
        inverse(i, 1)

    finish(first_load)
    repeat(lambda i: split(i, 0))
    finish(forward_load + second_load)
    repeat(second_split)
    finish(taps_load)
    for j in range(BLOCKS):
        multiply(j, j == 0)
        if j > 0:
            inverse(j - 1, 0)
    inverse(BLOCKS - 1, 0)
    stores += copies.start(cross_buf, cross_ref)
    repeat(first_gather)
    stores += copies.start(back_buf.at[0], back_ref.at[:, 0])
    for quarter in range(4):
        for i in range(quarter * 4, quarter * 4 + 4):
            gather(i, 1)
        rows = pl.ds(quarter * 2 * ROWS, 2 * ROWS)
        stores += copies.start(back_buf.at[1, :, rows], back_ref.at[:, 1, rows])
    finish(stores)


def transforms(fields, taps_spec, forward):
    count, _, rows, width = fields.shape
    block = (2 * INNER, width)
    return pl.pallas_call(
        transforms_kernel,
        in_specs=[HBM] * 3,
        out_specs=[HBM] * 2,
        out_shape=[
            jax.ShapeDtypeStruct(fields.shape, BF16),
            jax.ShapeDtypeStruct((BLOCKS,) + block, BF16),
        ],
        scratch_shapes=[
            pltpu.VMEM((2, count, rows, width), BF16),
            pltpu.VMEM((BLOCKS,) + block, BF16),
            pltpu.VMEM(forward.shape, BF16),
            pltpu.VMEM((2, BLOCKS) + block, BF16),
            pltpu.VMEM((BLOCKS,) + block, F32),
            pltpu.VMEM((2, BLOCKS) + block, BF16),
            pltpu.VMEM((BLOCKS,) + block, BF16),
            pltpu.VMEM((2, BLOCKS) + block, F32),
            pltpu.VMEM((2, count, rows, width), BF16),
            pltpu.SemaphoreType.DMA((16,)),
        ],
        compiler_params=pltpu.CompilerParams(vmem_limit_bytes=61 << 20),
        name="transforms",
    )(fields, taps_spec, forward)


def term_kernel(scale, cross_hbm, forward_hbm, *refs):
    targets = refs[:8]
    cross_ref, forward_ref, parts_ref, term_buf, sems = refs[8:]
    copies = Copies(sems)
    loads = copies.start(forward_hbm, forward_ref, 2) + copies.start(cross_hbm, cross_ref, 2)

    def store(n, rows, lanes, y):
        place = pl.ds(pl.multiple_of((n % 2) * INNER + rows.start, ROWS), ROWS)
        term_buf[n // 4, (n // 2) % 2, place, lanes] = (y * scale).astype(BF16)

    finish(loads)
    for j in range(BLOCKS):
        parts_ref[j] = backward(forward_ref[j], cross_ref[j])
    repeat(lambda i: gather_chunk(i, parts_ref, store))
    column, side = lax.axis_index("dp") // 2, lax.axis_index("dp") % 2
    stores = []
    for half in (1, 0):
        for turn in range(4):
            ref = targets[4 * half + turn]
            stores += copies.start(term_buf.at[(column + turn) % 4, (side + half) % 2], ref)
    finish(stores)


def filter_term(cross, forward, length):
    share = (length // 8, cross.shape[2])
    refs = pl.pallas_call(
        functools.partial(term_kernel, 2.0 / TOTAL / math.sqrt(length)),
        in_specs=[HBM] * 2,
        out_specs=[HBM] * 8,
        out_shape=[jax.ShapeDtypeStruct(share, BF16)] * 8,
        scratch_shapes=[
            pltpu.VMEM(cross.shape, BF16),
            pltpu.VMEM(forward.shape, BF16),
            pltpu.VMEM(cross.shape, F32),
            pltpu.VMEM((4, 2) + share, BF16),
            pltpu.SemaphoreType.DMA((12,)),
        ],
        compiler_params=pltpu.CompilerParams(vmem_limit_bytes=61 << 20),
        name="filter_term",
    )(cross, forward)
    return refs[:4], refs[4:]


def outputs_kernel(back_ref, cotangent_ref, signal_grad_ref, gate_grad_ref, gate_buf, sems):
    count = back_ref.shape[0]
    pieces = count // PARTS
    stores = []
    for piece in range(count):
        lanes = pl.ds(piece * CHANNELS, CHANNELS)
        stores.append(pltpu.make_async_copy(back_ref.at[piece, 0], signal_grad_ref.at[0, :, lanes], sems.at[piece]))
        stores[-1].start()
    for part in range(PARTS):
        for piece in range(part * pieces, (part + 1) * pieces):
            lanes = pl.ds(piece * CHANNELS, CHANNELS)
            gate_buf[:, lanes] = (cotangent_ref[0, :, lanes].astype(F32) * back_ref[piece, 1].astype(F32)).astype(BF16)
        lanes = pl.ds(part * pieces * CHANNELS, pieces * CHANNELS)
        stores.append(pltpu.make_async_copy(gate_buf.at[:, lanes], gate_grad_ref.at[0, :, lanes], sems.at[count + part]))
        stores[-1].start()
    for store in stores:
        store.wait()


def place_outputs(back, cotangent):
    return pl.pallas_call(
        outputs_kernel,
        in_specs=[VMEM, VMEM],
        out_specs=[HBM, HBM],
        out_shape=[jax.ShapeDtypeStruct(cotangent.shape, BF16)] * 2,
        scratch_shapes=[
            pltpu.VMEM(cotangent.shape[1:], BF16),
            pltpu.SemaphoreType.DMA((back.shape[0] + PARTS,)),
        ],
        compiler_params=pltpu.CompilerParams(vmem_limit_bytes=12 << 20),
        name="outputs",
    )(back, cotangent)


def sum_over_sequences(own, others):
    devices = lax.axis_size("dp")

    def round_y(terms):
        moved = [terms[0]]
        for turn in (2, 1, 3):
            moved.append(lax.ppermute(terms[turn], "dp", [(d, (d + 2 * turn) % devices) for d in range(devices)]))
        return sum(term.astype(F32) for term in moved)

    away = round_y(others).astype(BF16)
    other = lax.ppermute(away, "dp", [(d, d ^ 1) for d in range(devices)])
    return round_y(own), other


def local(signal, gate, cotangent, filter_taps):
    count = lax.axis_size("ctx")
    forward = section_tables()
    fields = lax.all_to_all(send_fields(signal, gate, cotangent, count), "ctx", 0, 0, tiled=True)
    taps_spec = taps_spectrum(filter_taps, forward)
    back, cross = transforms(fields, taps_spec, forward)
    back = lax.all_to_all(back, "ctx", 0, 0, tiled=True)
    keep, other = sum_over_sequences(*filter_term(cross, forward, filter_taps.shape[0]))
    signal_grad, gate_grad = place_outputs(back, cotangent)
    signal_grad, other = lax.optimization_barrier((signal_grad, other))
    return (signal_grad, gate_grad, keep + other.astype(F32))


def solution(mesh):
    in_specs = (P("dp", "ctx", None), P("dp", "ctx", None), P("dp", "ctx", None), P(None, "ctx"))
    out_specs = (P("dp", "ctx", None), P("dp", "ctx", None), P("dp", "ctx"))
    return jax.shard_map(local, mesh=mesh, in_specs=in_specs, out_specs=out_specs, check_vma=False)
```

```python
import functools
import math

import jax
import jax.numpy as jnp
import ml_dtypes
import numpy as np
from jax import lax
from jax.experimental import pallas as pl
from jax.experimental.pallas import tpu as pltpu
from jax.sharding import PartitionSpec as P

F32 = jnp.float32
BF16 = jnp.bfloat16
RADIX = 32
INNER = 128
TOTAL = RADIX * INNER
BLOCKS = RADIX // 2
ROOT_HALF = math.sqrt(0.5)
COS_EIGHTH = math.cos(math.pi / 8)
SIN_EIGHTH = math.sin(math.pi / 8)
TURNS = [(math.cos(math.pi * k / 16), math.sin(math.pi * k / 16)) for k in (1, 3, 5, 7)]
CHANNELS = 256
ROWS = 16
LANES = 128


def section_tables():
    column = np.arange(INNER)[None, :]
    forward = np.zeros((BLOCKS, 2 * INNER, 2 * INNER))
    half = INNER // 2
    row = np.arange(half)[:, None]
    for section in range(2):
        angle = 2 * np.pi * ((column * (RADIX * row + BLOCKS * section)) % TOTAL) / TOTAL
        place = slice(section * INNER, (section + 1) * INNER)
        forward[0, section * half : (section + 1) * half, place] = np.cos(angle)
        forward[0, INNER + section * half : INNER + (section + 1) * half, place] = -np.sin(angle)
    forward[0, INNER, :INNER] = np.cos(np.pi * column[0])
    row = np.arange(INNER)[:, None]
    for j in range(1, BLOCKS):
        angle = 2 * np.pi * ((column * (RADIX * row + j)) % TOTAL) / TOTAL
        forward[j] = np.block([[np.cos(angle), np.sin(angle)], [-np.sin(angle), np.cos(angle)]])
    return forward.astype(ml_dtypes.bfloat16)


def half_sections(y0, y2, y4, y6):
    t, q = ROOT_HALF * (y2 - y6), ROOT_HALF * (y2 + y6)
    return (y0 + t, -(y4 + q)), (y0 - t, y4 - q)


def odd_sections(x):
    x0, x1, x2, x3, x4, x5, x6, x7 = x
    (e1r, e1i), (e3r, e3i) = half_sections(x0, x2, x4, x6)
    (o1r, o1i), (o3r, o3i) = half_sections(x1, x3, x5, x7)
    m1r, m1i = COS_EIGHTH * o1r + SIN_EIGHTH * o1i, COS_EIGHTH * o1i - SIN_EIGHTH * o1r
    m3r, m3i = SIN_EIGHTH * o3r + COS_EIGHTH * o3i, SIN_EIGHTH * o3i - COS_EIGHTH * o3r
    return (e1r + m1r, e1i + m1i), (e3r + m3r, e3i + m3i), (e3r - m3r, m3i - e3i), (e1r - m1r, m1i - e1i)


def sections(x):
    a = [x[n] + x[n + 8] for n in range(8)]
    b = [x[n] - x[n + 8] for n in range(8)]
    c = [a[n] + a[n + 4] for n in range(4)]
    d = [a[n] - a[n + 4] for n in range(4)]
    even, odd = c[0] + c[2], c[1] + c[3]
    t, q = ROOT_HALF * (d[1] - d[3]), ROOT_HALF * (d[1] + d[3])
    out = [None] * 16
    out[0] = (even + odd, even - odd)
    out[4] = (d[0] + t, -(d[2] + q))
    out[8] = (c[0] - c[2], c[3] - c[1])
    out[12] = (d[0] - t, d[2] - q)
    out[2], out[6], out[10], out[14] = odd_sections(b)
    pairs = zip((1, 3, 5, 7), TURNS, odd_sections(x[0::2]), odd_sections(x[1::2]))
    for k, (cos, sin), (er, ei), (tr, ti) in pairs:
        mr, mi = cos * tr + sin * ti, cos * ti - sin * tr
        out[k] = (er + mr, ei + mi)
        out[16 - k] = (er - mr, mi - ei)
    return out


def half_gather(e1r, e1i, e3r, e3i):
    t, w = ROOT_HALF * (e1r - e3r), ROOT_HALF * (e1i + e3i)
    return e1r + e3r, t - w, e3i - e1i, -(t + w)


def odd_gather(v1, v3, v5, v7):
    e1r, e1i, m1r, m1i = v1[0] + v7[0], v1[1] - v7[1], v1[0] - v7[0], v1[1] + v7[1]
    e3r, e3i, m3r, m3i = v3[0] + v5[0], v3[1] - v5[1], v3[0] - v5[0], v3[1] + v5[1]
    o1r, o1i = COS_EIGHTH * m1r - SIN_EIGHTH * m1i, SIN_EIGHTH * m1r + COS_EIGHTH * m1i
    o3r, o3i = SIN_EIGHTH * m3r - COS_EIGHTH * m3i, COS_EIGHTH * m3r + SIN_EIGHTH * m3i
    y0, y2, y4, y6 = half_gather(e1r, e1i, e3r, e3i)
    y1, y3, y5, y7 = half_gather(o1r, o1i, o3r, o3i)
    return [y0, y1, y2, y3, y4, y5, y6, y7]


def gather_sections(v):
    even, odd = v[0][0] + v[0][1], v[0][0] - v[0][1]
    c = [even + v[8][0], odd - v[8][1], even - v[8][0], odd + v[8][1]]
    t, w = ROOT_HALF * (v[4][0] - v[12][0]), ROOT_HALF * (v[4][1] + v[12][1])
    d = [v[4][0] + v[12][0], t - w, v[12][1] - v[4][1], -(t + w)]
    a = [c[n] + d[n] for n in range(4)] + [c[n] - d[n] for n in range(4)]
    b = odd_gather(v[2], v[6], v[10], v[14])
    straight, turned = [], []
    for k, (cos, sin) in zip((1, 3, 5, 7), TURNS):
        (pr, pi), (qr, qi) = v[k], v[16 - k]
        mr, mi = pr - qr, pi + qi
        straight.append((pr + qr, pi - qi))
        turned.append((cos * mr - sin * mi, sin * mr + cos * mi))
    ye, yo = odd_gather(*straight), odd_gather(*turned)
    y = [part for both in zip(ye, yo) for part in both]
    return [a[n] + b[n] + y[n] for n in range(8)] + [a[n] - b[n] + y[n + 8] for n in range(8)]


HBM = pl.BlockSpec(memory_space=pltpu.HBM)
VMEM = pl.BlockSpec(memory_space=pltpu.VMEM)
PARTS = 4


def product_kernel(signal_ref, gate_ref, cotangent_ref, out_ref, fields, products, in_sems, out_sems):
    each = fields.shape[2] // PARTS
    pieces = each // CHANNELS
    loads = []
    for part in range(PARTS):
        lanes = pl.ds(part * each, each)
        for field, ref in enumerate((gate_ref, cotangent_ref, signal_ref)):
            loads.append(pltpu.make_async_copy(ref.at[0, :, lanes], fields.at[field, :, lanes], in_sems.at[part, field]))
            loads[-1].start()
    stores = []
    for part in range(PARTS):
        for field in range(2):
            loads[3 * part + field].wait()
        for piece in range(part * pieces, (part + 1) * pieces):
            lanes = pl.ds(piece * CHANNELS, CHANNELS)
            products[piece] = (fields[1, :, lanes].astype(F32) * fields[0, :, lanes].astype(F32)).astype(BF16)
        whole = pl.ds(part * pieces, pieces)
        stores.append(pltpu.make_async_copy(products.at[whole], out_ref.at[whole, 1], out_sems.at[part]))
        stores[-1].start()
        loads[3 * part + 2].wait()
        for piece in range(part * pieces, (part + 1) * pieces):
            lanes = pl.ds(piece * CHANNELS, CHANNELS)
            stores.append(pltpu.make_async_copy(fields.at[2, :, lanes], out_ref.at[piece, 0], out_sems.at[PARTS + piece]))
            stores[-1].start()
    for store in stores:
        store.wait()


def send_fields(signal, gate, cotangent, count):
    rows, width = signal.shape[1:]
    return pl.pallas_call(
        product_kernel,
        in_specs=[HBM] * 3,
        out_specs=HBM,
        out_shape=jax.ShapeDtypeStruct((count, 2, rows, width // count), BF16),
        scratch_shapes=[
            pltpu.VMEM((3, rows, width), BF16),
            pltpu.VMEM((count, rows, width // count), BF16),
            pltpu.SemaphoreType.DMA((PARTS, 3)),
            pltpu.SemaphoreType.DMA((PARTS + count,)),
        ],
        compiler_params=pltpu.CompilerParams(vmem_limit_bytes=60 << 20),
        name="product",
    )(signal, gate, cotangent)


def chunk_of(i):
    start = pl.multiple_of((i // 2) * ROWS, ROWS)
    lanes = pl.ds(pl.multiple_of((i % 2) * LANES, LANES), LANES)
    return pl.ds(start, ROWS), pl.ds(pl.multiple_of(INNER + start, ROWS), ROWS), lanes


def split_chunk(i, sections_ref, load):
    rows, low, lanes = chunk_of(i)
    x = [load(n, rows, lanes) for n in range(RADIX // 2)]
    for j, (real, imag) in enumerate(sections(x)):
        sections_ref[j, rows, lanes] = real.astype(BF16)
        sections_ref[j, low, lanes] = imag.astype(BF16)


def gather_chunk(i, parts_ref, store):
    rows, low, lanes = chunk_of(i)
    v = [(parts_ref[j, rows, lanes], parts_ref[j, low, lanes]) for j in range(BLOCKS)]
    for n, y in enumerate(gather_sections(v)):
        store(n, rows, lanes, y)


def repeat(step):
    def body(i, _):
        step(i)
        return 0

    lax.fori_loop(0, BLOCKS, body, 0, unroll=True)


def taps_kernel(scale, taps_ref, forward_ref, out_ref, sections_ref):
    def load(n, rows, lanes):
        return taps_ref[pl.ds(pl.multiple_of(n * INNER + rows.start, ROWS), ROWS), lanes] * scale

    repeat(lambda i: split_chunk(i, sections_ref, load))
    for j in range(BLOCKS):
        out_ref[j] = jnp.dot(forward_ref[j], sections_ref[j], preferred_element_type=F32).astype(BF16)


def taps_spectrum(taps, forward):
    length, width = taps.shape
    return pl.pallas_call(
        functools.partial(taps_kernel, 2.0 / TOTAL / math.sqrt(length)),
        in_specs=[VMEM, VMEM],
        out_specs=VMEM,
        out_shape=jax.ShapeDtypeStruct((BLOCKS, 2 * INNER, width), BF16),
        scratch_shapes=[pltpu.VMEM((BLOCKS, 2 * INNER, width), BF16)],
        compiler_params=pltpu.CompilerParams(vmem_limit_bytes=24 << 20),
        name="taps_spectrum",
    )(taps, forward)


def multiply_spectra(left, right, conjugate, lone):
    lr, li, rr, ri = left[:INNER], left[INNER:], right[:INNER], right[INNER:]
    if conjugate:
        pr, pi = lr * rr + li * ri, lr * ri - li * rr
    else:
        pr, pi = lr * rr - li * ri, lr * ri + li * rr
    if lone:
        first = lax.broadcasted_iota(jnp.int32, pr.shape, 0) == 0
        pr, pi = jnp.where(first, 0.5 * lr * rr, pr), jnp.where(first, 0.5 * li * ri, pi)
    return jnp.concatenate([pr.astype(BF16), pi.astype(BF16)], axis=0)


class Copies:
    def __init__(self, sems):
        self.sems, self.used = sems, 0

    def start(self, source, target, pieces=1):
        each = source.shape[0] // pieces
        copies = []
        for piece in range(pieces):
            part = pl.ds(piece * each, each)
            copies.append(pltpu.make_async_copy(source.at[part], target.at[part], self.sems.at[self.used]))
            copies[-1].start()
            self.used += 1
        return copies


def finish(copies):
    for copy in copies:
        copy.wait()


def backward(table, spectrum):
    return lax.dot_general(table, spectrum, (((0,), (0,)), ((), ())), preferred_element_type=F32)


def transforms_kernel(
    fields_hbm,
    taps_hbm,
    forward_hbm,
    back_ref,
    cross_ref,
    fields_ref,
    taps_ref,
    forward_ref,
    sections_ref,
    signal_ref,
    spectra_ref,
    cross_buf,
    parts_ref,
    back_buf,
    sems,
):
    copies = Copies(sems)
    first_load = []
    for part in range(PARTS):
        rows = pl.ds(part * (INNER // PARTS), INNER // PARTS)
        first_load += copies.start(fields_hbm.at[:, 0, rows], fields_ref.at[0, :, rows])
    second_load = copies.start(fields_hbm.at[:, 1], fields_ref.at[1], 2)
    forward_load = copies.start(forward_hbm, forward_ref, 2)
    taps_load = copies.start(taps_hbm, taps_ref, 2)
    stores = []

    def split(i, field):
        split_chunk(
            i, sections_ref.at[field], lambda n, rows, lanes: fields_ref[field, n, rows, lanes].astype(F32)
        )

    def gather(i, out):
        def store(n, rows, lanes, y):
            back_buf[out, n, rows, lanes] = y.astype(BF16)

        gather_chunk(i, parts_ref.at[out], store)

    def forward(j, field):
        return jnp.dot(forward_ref[j], sections_ref[field, j], preferred_element_type=F32)

    def inverse(j, out):
        parts_ref[out, j] = backward(forward_ref[j], spectra_ref[out, j])

    def multiply(j, lone):
        product, taps, signal = forward(j, 1), taps_ref[j].astype(F32), signal_ref[j]
        cross_buf[j] = multiply_spectra(signal, product, True, lone)
        spectra_ref[0, j] = multiply_spectra(taps, product, True, lone)
        spectra_ref[1, j] = multiply_spectra(taps, signal, False, lone)

    def second_split(i):
        split(i, 1)
        signal_ref[i] = forward(i, 0)

    def first_gather(i):
        gather(i, 0)
        inverse(i, 1)

    for i in range(BLOCKS):
        if i % (BLOCKS // PARTS) == 0:
            first_load[i // (BLOCKS // PARTS)].wait()
        split(i, 0)
    finish(forward_load + second_load)
    repeat(second_split)
    finish(taps_load)
    for j in range(BLOCKS):
        multiply(j, j == 0)
        if j > 0:
            inverse(j - 1, 0)
    inverse(BLOCKS - 1, 0)
    stores += copies.start(cross_buf, cross_ref)
    repeat(first_gather)
    stores += copies.start(back_buf.at[0], back_ref.at[:, 0])
    for quarter in range(4):
        for i in range(quarter * 4, quarter * 4 + 4):
            gather(i, 1)
        rows = pl.ds(quarter * 2 * ROWS, 2 * ROWS)
        stores += copies.start(back_buf.at[1, :, rows], back_ref.at[:, 1, rows])
    finish(stores)


def transforms(fields, taps_spec, forward):
    count, _, rows, width = fields.shape
    block = (2 * INNER, width)
    return pl.pallas_call(
        transforms_kernel,
        in_specs=[HBM] * 3,
        out_specs=[HBM] * 2,
        out_shape=[
            jax.ShapeDtypeStruct(fields.shape, BF16),
            jax.ShapeDtypeStruct((BLOCKS,) + block, BF16),
        ],
        scratch_shapes=[
            pltpu.VMEM((2, count, rows, width), BF16),
            pltpu.VMEM((BLOCKS,) + block, BF16),
            pltpu.VMEM(forward.shape, BF16),
            pltpu.VMEM((2, BLOCKS) + block, BF16),
            pltpu.VMEM((BLOCKS,) + block, F32),
            pltpu.VMEM((2, BLOCKS) + block, BF16),
            pltpu.VMEM((BLOCKS,) + block, BF16),
            pltpu.VMEM((2, BLOCKS) + block, F32),
            pltpu.VMEM((2, count, rows, width), BF16),
            pltpu.SemaphoreType.DMA((16,)),
        ],
        compiler_params=pltpu.CompilerParams(vmem_limit_bytes=61 << 20),
        name="transforms",
    )(fields, taps_spec, forward)


def term_kernel(scale, cross_hbm, forward_hbm, *refs):
    targets = refs[:8]
    cross_ref, forward_ref, parts_ref, term_buf, sems = refs[8:]
    copies = Copies(sems)
    loads = []
    for part in range(PARTS):
        blocks = pl.ds(part * (BLOCKS // PARTS), BLOCKS // PARTS)
        loads.append(
            copies.start(forward_hbm.at[blocks], forward_ref.at[blocks])
            + copies.start(cross_hbm.at[blocks], cross_ref.at[blocks])
        )

    def store(n, rows, lanes, y):
        place = pl.ds(pl.multiple_of((n % 2) * INNER + rows.start, ROWS), ROWS)
        term_buf[n // 4, (n // 2) % 2, place, lanes] = (y * scale).astype(BF16)

    for j in range(BLOCKS):
        if j % (BLOCKS // PARTS) == 0:
            finish(loads[j // (BLOCKS // PARTS)])
        parts_ref[j] = backward(forward_ref[j], cross_ref[j])
    repeat(lambda i: gather_chunk(i, parts_ref, store))
    column, side = lax.axis_index("dp") // 2, lax.axis_index("dp") % 2
    stores = []
    for half in (1, 0):
        for turn in range(4):
            ref = targets[4 * half + turn]
            stores += copies.start(term_buf.at[(column + turn) % 4, (side + half) % 2], ref)
    finish(stores)


def filter_term(cross, forward, length):
    share = (length // 8, cross.shape[2])
    refs = pl.pallas_call(
        functools.partial(term_kernel, 2.0 / TOTAL / math.sqrt(length)),
        in_specs=[HBM] * 2,
        out_specs=[HBM] * 8,
        out_shape=[jax.ShapeDtypeStruct(share, BF16)] * 8,
        scratch_shapes=[
            pltpu.VMEM(cross.shape, BF16),
            pltpu.VMEM(forward.shape, BF16),
            pltpu.VMEM(cross.shape, F32),
            pltpu.VMEM((4, 2) + share, BF16),
            pltpu.SemaphoreType.DMA((8 + 2 * PARTS,)),
        ],
        compiler_params=pltpu.CompilerParams(vmem_limit_bytes=61 << 20),
        name="filter_term",
    )(cross, forward)
    return refs[:4], refs[4:]


def outputs_kernel(back_ref, cotangent_ref, signal_grad_ref, gate_grad_ref, gate_buf, sems):
    count = back_ref.shape[0]
    pieces = count // PARTS
    stores = []
    for piece in range(count):
        lanes = pl.ds(piece * CHANNELS, CHANNELS)
        stores.append(pltpu.make_async_copy(back_ref.at[piece, 0], signal_grad_ref.at[0, :, lanes], sems.at[piece]))
        stores[-1].start()
    for part in range(PARTS):
        for piece in range(part * pieces, (part + 1) * pieces):
            lanes = pl.ds(piece * CHANNELS, CHANNELS)
            gate_buf[:, lanes] = (cotangent_ref[0, :, lanes].astype(F32) * back_ref[piece, 1].astype(F32)).astype(BF16)
        lanes = pl.ds(part * pieces * CHANNELS, pieces * CHANNELS)
        stores.append(pltpu.make_async_copy(gate_buf.at[:, lanes], gate_grad_ref.at[0, :, lanes], sems.at[count + part]))
        stores[-1].start()
    for store in stores:
        store.wait()


def place_outputs(back, cotangent):
    return pl.pallas_call(
        outputs_kernel,
        in_specs=[VMEM, VMEM],
        out_specs=[HBM, HBM],
        out_shape=[jax.ShapeDtypeStruct(cotangent.shape, BF16)] * 2,
        scratch_shapes=[
            pltpu.VMEM(cotangent.shape[1:], BF16),
            pltpu.SemaphoreType.DMA((back.shape[0] + PARTS,)),
        ],
        compiler_params=pltpu.CompilerParams(vmem_limit_bytes=12 << 20),
        name="outputs",
    )(back, cotangent)


def sum_over_sequences(own, others):
    devices = lax.axis_size("dp")

    def round_y(terms):
        moved = [terms[0]]
        for turn in (2, 1, 3):
            moved.append(lax.ppermute(terms[turn], "dp", [(d, (d + 2 * turn) % devices) for d in range(devices)]))
        return sum(term.astype(F32) for term in moved)

    away = round_y(others).astype(BF16)
    other = lax.ppermute(away, "dp", [(d, d ^ 1) for d in range(devices)])
    return round_y(own), other


def local(signal, gate, cotangent, filter_taps):
    count = lax.axis_size("ctx")
    forward = section_tables()
    fields = lax.all_to_all(send_fields(signal, gate, cotangent, count), "ctx", 0, 0, tiled=True)
    taps_spec = taps_spectrum(filter_taps, forward)
    back, cross = transforms(fields, taps_spec, forward)
    back = lax.all_to_all(back, "ctx", 0, 0, tiled=True)
    keep, other = sum_over_sequences(*filter_term(cross, forward, filter_taps.shape[0]))
    signal_grad, gate_grad = place_outputs(back, cotangent)
    signal_grad, other = lax.optimization_barrier((signal_grad, other))
    return (signal_grad, gate_grad, keep + other.astype(F32))


def solution(mesh):
    in_specs = (P("dp", "ctx", None), P("dp", "ctx", None), P("dp", "ctx", None), P(None, "ctx"))
    out_specs = (P("dp", "ctx", None), P("dp", "ctx", None), P("dp", "ctx"))
    return jax.shard_map(local, mesh=mesh, in_specs=in_specs, out_specs=out_specs, check_vma=False)
```
